128 devices in a mesh: clus: 2 (over core), help: 64 (over z, y, x).
Axes of the slice: x: 4, y: 4, z: 4, core: 2. Of those that a mesh axis runs over, the one named last changes fastest.
Arguments:
- embeddings: bfloat16 [2, 64, 512, 1024], P('clus', 'help'), may hold values from -100 to 100, as said below
- row_mask: int32 [2, 64, 512], P('clus', 'help'), may hold values 0 or 1
- tile_counts: int32 [2], P('clus'), may hold values from 1 to 64, as said below
Outputs:
- max_similarity: float32 [2, 64, 512], P('clus', 'help')
The draws below stay inside these ranges and needn't reach their ends.
Inputs may be any that keep to these rules, and one draw needn't show every extreme that they name: `embeddings`: finite values; rows of any scale. `tile_counts`: some cluster has all 64 tiles live.
All inputs are finite; a program needn't handle non-finite values. No bound on the sum of `row_mask` on one device may be relied on, other than what follows from the above.
Results may differ from the reference program's by a relative error of at most 0.00054.
Values may be sent and summed in bfloat16 or wider, within the bound.
No kernel may reach another device: no remote copies, remote signals or barrier semaphores. Data moves between devices by JAX's collectives and lax.ppermute only.
A program may use at most 192 MiB of HBM per device.

```python
import jax
import jax.numpy as jnp
from jax import lax

E = 1024
TR = 512
TILES = 64
CLUSTERS = 2


def draw_embeddings(key, part):
    key = jax.random.fold_in(key, 11)
    base_key, mix_key, partner_key = jax.random.split(key, 3)
    total_rows = TILES * TR
    base = jnp.clip(jax.random.normal(base_key, (CLUSTERS, total_rows, E), jnp.float32), -6.0, 6.0)
    position = jnp.arange(total_rows, dtype=jnp.int32)
    raw_pick = jax.random.randint(partner_key, (CLUSTERS, total_rows), 0, 1073741824, dtype=jnp.int32)
    partner = raw_pick % jnp.maximum(position, 1)[None, :]
    partnered = jnp.take_along_axis(base, partner[:, :, None], axis=1)
    mixing = jnp.exp(jax.random.uniform(mix_key, (CLUSTERS, total_rows, 1), jnp.float32, jnp.log(0.2), jnp.log(3.0)))
    values = base + mixing * partnered
    return values.reshape(CLUSTERS, TILES, TR, E).astype(jnp.bfloat16)


def draw_tile_counts(key, part):
    key = jax.random.fold_in(key, 23)
    count_key, pick_key = jax.random.split(key)
    counts = jax.random.randint(count_key, (CLUSTERS,), 1, TILES, dtype=jnp.int32)
    chosen = jax.random.randint(pick_key, (), 0, CLUSTERS, dtype=jnp.int32)
    return jnp.where(jnp.arange(CLUSTERS, dtype=jnp.int32) == chosen, jnp.int32(TILES), counts)


def touch_ends(drawn, own_key, low, high):
    longest = drawn.shape.index(max(drawn.shape))
    spots = []
    for shift in (0, 1):
        where = [jax.random.randint(jax.random.fold_in(own_key, axis), (), 0, length) for axis, length in enumerate(drawn.shape)]
        where[longest] = (where[longest] + shift) % drawn.shape[longest]
        spots.append(tuple(where))
    return drawn.at[spots[0]].set(low).at[spots[1]].set(high)


def setup_inputs(seed: int = 0) -> dict:
    arg_keys = jax.random.split(jax.random.key(seed), 4)
    return {
        "embeddings": draw_embeddings(jax.random.fold_in(arg_keys[3], 71), 0),
        "row_mask": touch_ends((jax.random.randint(arg_keys[1], (CLUSTERS, TILES, TR), 0, 8) < 7).astype(jnp.int32), jax.random.fold_in(arg_keys[1], 1), 0, 1),
        "tile_counts": draw_tile_counts(jax.random.fold_in(arg_keys[3], 71), 0),
    }


EPS = 1e-06

def unit_rows(values):
    widths = values.astype(jnp.float32)
    meansq = lax.optimization_barrier(jnp.mean(widths * widths, axis=-1, keepdims=True))
    scaled = widths * lax.rsqrt(meansq + EPS) * (1.0 / values.shape[-1] ** 0.5)
    return scaled.astype(jnp.bfloat16)

def reference(embeddings, row_mask, tile_counts):

    def one_cluster(items):
        block, marks, count = items
        units = unit_rows(block).astype(jnp.float32).reshape(TILES * TR, E)
        position = jnp.arange(TILES * TR, dtype=jnp.int32)
        tile_of = position // TR
        live = (marks.reshape(-1) == 1) & (tile_of < count)
        sims = jnp.dot(units, units.T, precision=lax.Precision.HIGHEST, preferred_element_type=jnp.float32)
        allowed = (position[None, :] < position[:, None]) & live[None, :]
        best = lax.optimization_barrier(jnp.max(jnp.where(allowed, sims, jnp.float32(-1.0)), axis=1))
        return best.reshape(TILES, TR)
    return lax.map(one_cluster, (embeddings, row_mask, tile_counts))
```

```python
import functools

import jax
import jax.numpy as jnp
import numpy as np
from jax import lax
from jax.experimental import pallas as pl
from jax.experimental.pallas import tpu as pltpu
from jax.sharding import PartitionSpec as P

EPS = 1e-06
SIDE = 4
FLAG_ROWS = 16
DEAD = -4.0

PLAN = [
    ((1, 0, 0), (0, 0, 0)),
    ((3, 0, 1), (0, 0, 0)),
    ((0, 1, 0), (0, 0, 0)),
    ((0, 3, 3), (0, 0, 0)),
    ((1, 1, 0), (1, 0, 0)),
    ((0, 3, 0), (0, 0, 0)),
    ((3, 0, 2), (3, 0, 1)),
    ((3, 3, 3), (0, 3, 3)),
    ((0, 3, 2), (0, 3, 3)),
    ((2, 1, 0), (1, 1, 0)),
]
OFFSETS = [(0, 0, 0)] + [d for d, _ in PLAN]
STAGES = [2, 4, 6, 8, 10]


def turned(d):
    return (d[1], d[0], -d[2])


def place_of(v):
    return ((v[0] % SIDE) * SIDE + v[1] % SIDE) * SIDE + v[2] % SIDE


def cube():
    return [(z, y, x) for z in range(SIDE) for y in range(SIDE) for x in range(SIDE)]


def add(a, b):
    return tuple(x + y for x, y in zip(a, b))


def sub(a, b):
    return tuple((x - y) % SIDE for x, y in zip(a, b))


def moves(step):
    pairs = []
    for c in range(2):
        s = turned(step) if c else step
        for v in cube():
            pairs.append((c * SIDE**3 + place_of(add(v, s)), c * SIDE**3 + place_of(v)))
    return pairs


def choose_pairs():
    best = {}
    for a in range(len(OFFSETS)):
        for b in range(a):
            g = sub(OFFSETS[a], OFFSETS[b])
            key = min(g, sub((0, 0, 0), g))
            if key not in best:
                best[key] = (a, b)
    assert len(best) == (SIDE**3 - 1 + 7) // 2
    return sorted(best.values())


def work_table():
    stages = [[] for _ in STAGES]
    for a, b in choose_pairs():
        stage = next(i for i, n in enumerate(STAGES) if a <= n)
        twin = all((2 * g) % SIDE == 0 for g in sub(OFFSETS[a], OFFSETS[b]))
        stages[stage].extend([(a, b, -1)] if twin else [(a, b, 0), (a, b, 1)])
    units = [u for s in stages for u in s]
    table = np.zeros((2, SIDE**3, len(units) * 3), np.int32)
    for c in range(2):
        offs = [turned(d) if c else d for d in OFFSETS]
        for v in cube():
            for n, (a, b, half) in enumerate(units):
                first = place_of(add(v, offs[a])) < place_of(add(v, offs[b]))
                k, q = (a, b) if first else (b, a)
                h = half if half >= 0 else int(first)
                table[c, place_of(v), 3 * n : 3 * n + 3] = (k, q, h)
    return table, [len(s) for s in stages], stages


def unit_kernel(alive, x_ref, mask_ref, out_ref):
    rows, width = x_ref.shape
    x = x_ref[...].astype(jnp.float32)
    meansq = jnp.mean(x * x, axis=-1, keepdims=True)
    out_ref[:rows, :] = (x * lax.rsqrt(meansq + EPS) * (1.0 / width**0.5)).astype(jnp.bfloat16)
    live = (mask_ref[...] == 1) & (alive[0] == 1)
    bias = jnp.broadcast_to(jnp.where(live, 0.0, DEAD), (FLAG_ROWS, rows))
    top = lax.broadcasted_iota(jnp.int32, (FLAG_ROWS, rows), 0) == 0
    out_ref[rows:, :] = jnp.zeros((FLAG_ROWS, width), jnp.bfloat16)
    out_ref[rows:, :rows] = jnp.where(top, bias, 0.0).astype(jnp.bfloat16)


def dot_t(a, b):
    return lax.dot_general(a, b, (((1,), (1,)), ((), ())), preferred_element_type=jnp.float32)


def key_bias(flags):
    ones = jnp.ones((flags.shape[0], 128), jnp.bfloat16)
    return lax.dot_general(flags, ones, (((0,), (0,)), ((), ())), preferred_element_type=jnp.float32)


def fold_rows(s):
    n, w = s.shape
    return jnp.max(s.reshape(n // 8, 8, w), axis=0)


def self_kernel(t_ref, acc_ref, *, slots):
    rows = t_ref.shape[0] - FLAG_ROWS
    half = rows // 2
    bias = key_bias(t_ref[rows:, :rows])
    acc_ref[...] = jnp.full(acc_ref.shape, -1.0, jnp.float32)
    for h in range(2):
        n = half * (h + 1)
        s = dot_t(t_ref[:n, :], t_ref[h * half : (h + 1) * half, :])
        key = lax.broadcasted_iota(jnp.int32, (n, half), 0)
        query = lax.broadcasted_iota(jnp.int32, (n, half), 1) + h * half
        s = jnp.where(key < query, s + jnp.tile(bias[:n], (1, half // 128)), -1.0)
        acc_ref[0, h] = jnp.maximum(acc_ref[0, h], fold_rows(s))


def pair_kernel(tab, *refs, slots, first, stage_units, last):
    n = len(slots)
    tiles, acc_in, outs = refs[:n], refs[n], refs[n + 1 : -4]
    stack, biases, acc, sems = refs[-4:]
    rows = stack.shape[1] - FLAG_ROWS
    half = rows // 2
    order = sorted(range(n), key=lambda i: first[i])
    for i in order:
        pltpu.make_async_copy(tiles[i], stack.at[slots[i]], sems.at[i]).start()
    acc[...] = acc_in[...]
    start, count = stage_units

    def unit(u, carry):
        for i in range(n):

            @pl.when(u == first[i])
            def _():
                pltpu.make_async_copy(tiles[i], stack.at[slots[i]], sems.at[i]).wait()
                biases[slots[i]] = key_bias(stack[slots[i], rows:, :rows])

        at = 3 * (start + u)
        k, q, h = tab[at], tab[at + 1], tab[at + 2]
        query = stack[q, pl.ds(pl.multiple_of(h * half, half), half), :]
        s = dot_t(stack[k, :rows, :], query)
        s = s + jnp.tile(biases[k], (1, half // 128))
        acc[q, h] = jnp.maximum(acc[q, h], fold_rows(s))
        return carry

    lax.fori_loop(0, count, unit, 0)
    if last:
        for s in range(acc.shape[0]):
            for h in range(2):
                outs[s][:, h * half : (h + 1) * half] = jnp.max(acc[s, h], axis=0, keepdims=True)
    else:
        outs[0][...] = acc[...]


def on_device(embeddings, row_mask, tile_counts):
    rows, width = embeddings.shape[2:]
    half = rows // 2
    clus, place = lax.axis_index("clus"), lax.axis_index("help")
    table, unit_counts, stages = work_table()
    tab = jnp.asarray(table)[clus, place]
    alive = (place < tile_counts).astype(jnp.int32)
    slots = len(OFFSETS)
    vmem, smem, hbm = (pl.BlockSpec(memory_space=m) for m in (pltpu.VMEM, pltpu.SMEM, pl.ANY))
    tile_shape = (rows + FLAG_ROWS, width)
    acc_shape = (slots, 2, 8, half)

    own = pl.pallas_call(
        unit_kernel,
        out_shape=jax.ShapeDtypeStruct(tile_shape, jnp.bfloat16),
        in_specs=[smem, vmem, vmem],
        out_specs=vmem,
    )(alive, embeddings[0, 0], row_mask[0])
    held = {OFFSETS[0]: own}
    for d, source in PLAN:
        held[d] = lax.ppermute(held[source], ("clus", "help"), moves(sub(d, source)))

    acc = pl.pallas_call(
        functools.partial(self_kernel, slots=slots),
        out_shape=jax.ShapeDtypeStruct(acc_shape, jnp.float32),
        in_specs=[vmem],
        out_specs=vmem,
        cost_estimate=pl.CostEstimate(flops=2 * rows * rows * width, bytes_accessed=2 * rows * width, transcendentals=0),
    )(own)
    start = 0
    for i, units in enumerate(stages):
        used = sorted({s for a, b, _ in units for s in (a, b)})
        first = [next(n for n, u in enumerate(units) if s in u[:2]) for s in used]
        last = i == len(stages) - 1
        shapes = [(1, rows)] * slots if last else [acc_shape]
        acc = pl.pallas_call(
            functools.partial(pair_kernel, slots=used, first=first, stage_units=(start, len(units)), last=last),
            out_shape=[jax.ShapeDtypeStruct(s, jnp.float32) for s in shapes],
            in_specs=[smem] + [hbm] * len(used) + [vmem],
            out_specs=[vmem] * len(shapes),
            scratch_shapes=[
                pltpu.VMEM((slots, *tile_shape), jnp.bfloat16),
                pltpu.VMEM((slots, rows, 128), jnp.float32),
                pltpu.VMEM(acc_shape, jnp.float32),
                pltpu.SemaphoreType.DMA((len(used),)),
            ],
            compiler_params=pltpu.CompilerParams(vmem_limit_bytes=32 * 2**20),
            cost_estimate=pl.CostEstimate(
                flops=len(units) * rows * rows * width, bytes_accessed=2 * len(used) * rows * width, transcendentals=0
            ),
        )(tab, *[held[OFFSETS[s]] for s in used], *([acc] if i == 0 else acc))
        start += len(units)
    best = acc[0]
    for s in range(1, slots):
        best = jnp.maximum(best, lax.ppermute(acc[s], ("clus", "help"), moves(sub((0, 0, 0), OFFSETS[s]))))
    return best[None]


def solution(mesh):
    in_specs = (P("clus", "help", None, None), P("clus", "help", None), P("clus"))
    out_specs = P("clus", "help", None)
    return jax.shard_map(on_device, mesh=mesh, in_specs=in_specs, out_specs=out_specs, check_vma=False)
```

```python
import functools

import jax
import jax.numpy as jnp
import numpy as np
from jax import lax
from jax.experimental import pallas as pl
from jax.experimental.pallas import tpu as pltpu
from jax.sharding import PartitionSpec as P

EPS = 1e-06
SIDE = 4
UNROLL = 8
FLAG_ROWS = 16
DEAD = -4.0
NORM_PARTS = 4

PLAN = [
    ((0, 1, 0), (0, 0, 0)),
    ((3, 0, 1), (0, 0, 0)),
    ((1, 0, 0), (0, 0, 0)),
    ((0, 3, 3), (0, 0, 0)),
    ((1, 1, 0), (0, 1, 0)),
    ((0, 3, 0), (0, 0, 0)),
    ((3, 0, 2), (3, 0, 1)),
    ((0, 3, 2), (0, 3, 3)),
    ((3, 3, 3), (0, 3, 3)),
    ((2, 1, 0), (1, 1, 0)),
]
OFFSETS = [(0, 0, 0)] + [d for d, _ in PLAN]
STAGES = [4, 6, 8, 10]


def turned(d):
    return (d[1], d[0], -d[2])


def place_of(v):
    return ((v[0] % SIDE) * SIDE + v[1] % SIDE) * SIDE + v[2] % SIDE


def cube():
    return [(z, y, x) for z in range(SIDE) for y in range(SIDE) for x in range(SIDE)]


def add(a, b):
    return tuple(x + y for x, y in zip(a, b))


def sub(a, b):
    return tuple((x - y) % SIDE for x, y in zip(a, b))


def moves(step):
    pairs = []
    for c in range(2):
        s = turned(step) if c else step
        for v in cube():
            pairs.append((c * SIDE**3 + place_of(add(v, s)), c * SIDE**3 + place_of(v)))
    return pairs


def choose_pairs():
    best = {}
    for a in range(len(OFFSETS)):
        for b in range(a):
            g = sub(OFFSETS[a], OFFSETS[b])
            key = min(g, sub((0, 0, 0), g))
            if key not in best:
                best[key] = (a, b)
    assert len(best) == (SIDE**3 - 1 + 7) // 2
    return sorted(best.values())


def work_table():
    stages = [[] for _ in STAGES]
    for a, b in choose_pairs():
        stage = next(i for i, n in enumerate(STAGES) if a <= n)
        twin = all((2 * g) % SIDE == 0 for g in sub(OFFSETS[a], OFFSETS[b]))
        stages[stage].extend([(a, b, -1)] if twin else [(a, b, 0), (a, b, 1)])
    loops = []
    for s in stages:
        steps = -(-len(s) // UNROLL)
        unroll = -(-len(s) // steps)
        loops.append((steps, unroll))
        s.extend([s[-1]] * (steps * unroll - len(s)))
    units = [u for s in stages for u in s]
    table = np.zeros((2, SIDE**3, len(OFFSETS) + len(units) * 3), np.int32)
    for c in range(2):
        offs = [turned(d) if c else d for d in OFFSETS]
        for v in cube():
            table[c, place_of(v), : len(OFFSETS)] = [place_of(add(v, d)) for d in offs]
            for n, (a, b, half) in enumerate(units):
                first = place_of(add(v, offs[a])) < place_of(add(v, offs[b]))
                k, q = (a, b) if first else (b, a)
                h = half if half >= 0 else int(first)
                at = len(OFFSETS) + 3 * n
                table[c, place_of(v), at : at + 3] = (k, q, h)
    return table, loops


def unit_kernel(alive, x_hbm, mask_hbm, out_ref, x_ref, mask_ref, sems):
    rows, width = x_ref.shape
    part = rows // NORM_PARTS
    copies = []
    for i in range(NORM_PARTS):
        at = pl.ds(i * part, part)
        copies.append(pltpu.make_async_copy(x_hbm.at[at], x_ref.at[at], sems.at[i]))
        copies[-1].start()
    copies.append(pltpu.make_async_copy(mask_hbm, mask_ref, sems.at[NORM_PARTS]))
    copies[-1].start()
    copies[-1].wait()
    live = (mask_ref[...] == 1) & (alive[0] == 1)
    bias = jnp.broadcast_to(jnp.where(live, 0.0, DEAD), (FLAG_ROWS, rows))
    top = lax.broadcasted_iota(jnp.int32, (FLAG_ROWS, rows), 0) == 0
    out_ref[rows:, :] = jnp.zeros((FLAG_ROWS, width), jnp.bfloat16)
    out_ref[rows:, :rows] = jnp.where(top, bias, 0.0).astype(jnp.bfloat16)
    for i in range(NORM_PARTS):
        copies[i].wait()
        at = slice(i * part, (i + 1) * part)
        x = x_ref[at, :].astype(jnp.float32)
        meansq = jnp.mean(x * x, axis=-1, keepdims=True)
        out_ref[at, :] = (x * lax.rsqrt(meansq + EPS) * (1.0 / width**0.5)).astype(jnp.bfloat16)


def dot_t(a, b):
    return lax.dot_general(a, b, (((1,), (1,)), ((), ())), preferred_element_type=jnp.float32)


def key_bias(flags):
    ones = jnp.ones((flags.shape[0], 128), jnp.bfloat16)
    return lax.dot_general(flags, ones, (((0,), (0,)), ((), ())), preferred_element_type=jnp.float32)


def fold_rows(s):
    n, w = s.shape
    return jnp.max(s.reshape(n // 8, 8, w), axis=0)


def unit_work(tab, at, stack, biases, acc):
    half = stack.shape[1] // 2
    k, q, h = tab[at], tab[at + 1], tab[at + 2]
    s = dot_t(stack[k], stack[q, pl.ds(pl.multiple_of(h * half, half), half), :])
    s = s + jnp.tile(biases[k], (1, half // 128))
    acc[q, h] = jnp.maximum(acc[q, h], fold_rows(s))


def self_kernel(t_ref, tab, stack, biases, acc, turn):
    rows = stack.shape[1]
    half = rows // 2
    stack[0] = t_ref[:rows, :]
    biases[0] = key_bias(t_ref[rows:, :rows])
    acc[...] = jnp.full(acc.shape, -1.0, jnp.float32)
    for h in range(2):
        n = half * (h + 1)
        s = dot_t(t_ref[:n, :], t_ref[h * half : (h + 1) * half, :])
        key = lax.broadcasted_iota(jnp.int32, (n, half), 0)
        query = lax.broadcasted_iota(jnp.int32, (n, half), 1) + h * half
        s = jnp.where(key < query, s + jnp.tile(biases[0, :n], (1, half // 128)), -1.0)
        acc[0, h] = jnp.maximum(acc[0, h], fold_rows(s))
    turn[...] = jnp.full(turn.shape, tab[0], jnp.int32)


def pair_kernel(tab, turn, *refs, new, start, steps, unroll, last):
    n = len(new)
    tiles = refs[:n]
    n_out = int(last)
    stack, biases, acc = refs[n + 3 : n + 6]
    outs = refs[n + 6 : n + 6 + n_out]
    sems = refs[n + 6 + n_out]
    rows = stack.shape[1]
    half = rows // 2
    copies = []
    for i, slot in enumerate(new):
        copies.append(pltpu.make_async_copy(tiles[i].at[pl.ds(0, rows)], stack.at[slot], sems.at[i]))
    for c in copies:
        c.start()
    for i, slot in enumerate(new):
        biases[slot] = key_bias(tiles[i][rows:, :rows])
    for c in copies:
        c.wait()

    def step(u, carry):
        for j in range(unroll):
            unit_work(tab, len(OFFSETS) + 3 * (start + u * unroll + j), stack, biases, acc)
        return carry

    lax.fori_loop(0, steps, step, 0)
    if last:
        outs[0][...] = jnp.full(outs[0].shape, -1.0, jnp.float32)
        for s in range(acc.shape[0]):
            for h in range(2):
                outs[0][pl.ds(tab[s], 1), h * half : (h + 1) * half] = jnp.max(acc[s, h], axis=0, keepdims=True)


def on_device(embeddings, row_mask, tile_counts):
    rows, width = embeddings.shape[2:]
    half = rows // 2
    clus, place = lax.axis_index("clus"), lax.axis_index("help")
    table, loops = work_table()
    tab = jnp.asarray(table)[clus, place]
    alive = (place < tile_counts).astype(jnp.int32)
    slots = len(OFFSETS)
    vmem, smem, hbm = (pl.BlockSpec(memory_space=m) for m in (pltpu.VMEM, pltpu.SMEM, pltpu.HBM))
    state = [
        pltpu.VMEM((slots, rows, width), jnp.bfloat16),
        pltpu.VMEM((slots, rows, 128), jnp.float32),
        pltpu.VMEM((slots, 2, 8, half), jnp.float32),
    ]

    own = pl.pallas_call(
        unit_kernel,
        out_shape=pltpu.VMEM((rows + FLAG_ROWS, width), jnp.bfloat16),
        in_specs=[smem, hbm, hbm],
        out_specs=vmem,
        scratch_shapes=[
            pltpu.VMEM((rows, width), jnp.bfloat16),
            pltpu.VMEM((1, rows), jnp.int32),
            pltpu.SemaphoreType.DMA((NORM_PARTS + 1,)),
        ],
        compiler_params=pltpu.CompilerParams(vmem_limit_bytes=24 * 2**20),
    )(alive, embeddings[0, 0], row_mask[0])
    *held_state, turn = pl.pallas_call(
        self_kernel,
        out_shape=state + [jax.ShapeDtypeStruct((8, 128), jnp.int32)],
        in_specs=[vmem, smem],
        out_specs=[vmem] * 4,
        compiler_params=pltpu.CompilerParams(vmem_limit_bytes=24 * 2**20),
        cost_estimate=pl.CostEstimate(flops=1000, bytes_accessed=1000, transcendentals=0),
    )(own, tab)
    held = {OFFSETS[0]: own}
    for d, source in PLAN:
        if source != OFFSETS[0] and source == PLAN[0][0]:
            held[source], turn = lax.optimization_barrier((held[source], turn))
        held[d] = lax.ppermute(held[source], ("clus", "help"), moves(sub(d, source)))

    start, arrived = 0, 0
    for i, (steps, unroll) in enumerate(loops):
        new = list(range(arrived + 1, STAGES[i] + 1))
        last = i == len(loops) - 1
        outs = [jax.ShapeDtypeStruct((SIDE**3, rows), jnp.float32)] * int(last)
        results = pl.pallas_call(
            functools.partial(pair_kernel, new=new, start=start, steps=steps, unroll=unroll, last=last),
            out_shape=state + outs,
            in_specs=[smem] + [vmem] * (len(new) + 4),
            out_specs=[vmem] * (3 + len(outs)),
            input_output_aliases={2 + len(new) + j: j for j in range(3)},
            scratch_shapes=[pltpu.SemaphoreType.DMA((len(new),))],
            compiler_params=pltpu.CompilerParams(vmem_limit_bytes=24 * 2**20),
            cost_estimate=pl.CostEstimate(
                flops=1000, bytes_accessed=1000, transcendentals=0
            ),
        )(tab, turn, *[held[OFFSETS[s]] for s in new], *held_state)
        held_state, finals = results[:3], results[3:]
        start += steps * unroll
        arrived = STAGES[i]
    parts = lax.all_to_all(finals[0], "help", 0, 0, tiled=True)
    return jnp.max(parts, axis=0)[None, None]


def solution(mesh):
    in_specs = (P("clus", "help", None, None), P("clus", "help", None), P("clus"))
    out_specs = P("clus", "help", None)
    return jax.shard_map(on_device, mesh=mesh, in_specs=in_specs, out_specs=out_specs, check_vma=False)
```

```python
import functools

import jax
import jax.numpy as jnp
import numpy as np
from jax import lax
from jax.experimental import pallas as pl
from jax.experimental.pallas import tpu as pltpu
from jax.sharding import PartitionSpec as P

EPS = 1e-06
SIDE = 4
UNROLL = 12
FLAG_ROWS = 16
DEAD = -4.0
NORM_PARTS = 4

PLAN = [
    ((0, 0, 1), (0, 0, 0)),
    ((3, 1, 0), (0, 0, 0)),
    ((0, 3, 1), (0, 0, 1)),
    ((1, 0, 0), (0, 0, 0)),
    ((3, 0, 3), (0, 0, 0)),
    ((3, 1, 3), (3, 1, 0)),
    ((3, 1, 1), (3, 1, 0)),
    ((1, 3, 1), (0, 3, 1)),
    ((1, 1, 0), (1, 0, 0)),
    ((3, 3, 3), (3, 0, 3)),
]
OFFSETS = [(0, 0, 0)] + [d for d, _ in PLAN]
STAGES = [2, 5, 7, 9, 10]
GATES = {(0, 3, 1): 0, (1, 3, 1): 1}
AFTER = {(1, 0, 0): (0, 0, 1), (3, 0, 3): (0, 0, 1)}


def turned(d):
    return (-d[0], -d[2], -d[1])


def place_of(v):
    return ((v[0] % SIDE) * SIDE + v[1] % SIDE) * SIDE + v[2] % SIDE


def cube():
    return [(z, y, x) for z in range(SIDE) for y in range(SIDE) for x in range(SIDE)]


def add(a, b):
    return tuple(x + y for x, y in zip(a, b))


def sub(a, b):
    return tuple((x - y) % SIDE for x, y in zip(a, b))


def moves(step):
    pairs = []
    for c in range(2):
        s = turned(step) if c else step
        for v in cube():
            pairs.append((c * SIDE**3 + place_of(add(v, s)), c * SIDE**3 + place_of(v)))
    return pairs


def choose_pairs():
    best = {}
    for a in range(len(OFFSETS)):
        for b in range(a):
            g = sub(OFFSETS[a], OFFSETS[b])
            key = min(g, sub((0, 0, 0), g))
            if key not in best:
                best[key] = (a, b)
    assert len(best) == (SIDE**3 - 1 + 7) // 2
    return sorted(best.values())


def work_table():
    stages = [[] for _ in STAGES]
    for a, b in choose_pairs():
        stage = next(i for i, n in enumerate(STAGES) if a <= n)
        twin = all((2 * g) % SIDE == 0 for g in sub(OFFSETS[a], OFFSETS[b]))
        stages[stage].extend([(a, b, -1)] if twin else [(a, b, 0), (a, b, 1)])
    loops = []
    for s in stages:
        steps = -(-len(s) // UNROLL)
        unroll = -(-len(s) // steps)
        loops.append((steps, unroll))
        s.extend([s[-1]] * (steps * unroll - len(s)))
    units = [u for s in stages for u in s]
    table = np.zeros((2, SIDE**3, len(OFFSETS) + len(units) * 3), np.int32)
    for c in range(2):
        offs = [turned(d) if c else d for d in OFFSETS]
        for v in cube():
            table[c, place_of(v), : len(OFFSETS)] = [place_of(add(v, d)) for d in offs]
            for n, (a, b, half) in enumerate(units):
                first = place_of(add(v, offs[a])) < place_of(add(v, offs[b]))
                k, q = (a, b) if first else (b, a)
                h = half if half >= 0 else int(first)
                at = len(OFFSETS) + 3 * n
                table[c, place_of(v), at : at + 3] = (k, q, h)
    return table, loops


def unit_kernel(alive, x_hbm, mask_hbm, out_ref, x_ref, mask_ref, sems):
    rows, width = x_ref.shape
    part = rows // NORM_PARTS
    copies = []
    for i in range(NORM_PARTS):
        at = pl.ds(i * part, part)
        copies.append(pltpu.make_async_copy(x_hbm.at[at], x_ref.at[at], sems.at[i]))
        copies[-1].start()
    copies.append(pltpu.make_async_copy(mask_hbm, mask_ref, sems.at[NORM_PARTS]))
    copies[-1].start()
    copies[-1].wait()
    live = (mask_ref[...] == 1) & (alive[0] == 1)
    bias = jnp.broadcast_to(jnp.where(live, 0.0, DEAD), (FLAG_ROWS, rows))
    top = lax.broadcasted_iota(jnp.int32, (FLAG_ROWS, rows), 0) == 0
    out_ref[rows:, :] = jnp.zeros((FLAG_ROWS, width), jnp.bfloat16)
    out_ref[rows:, :rows] = jnp.where(top, bias, 0.0).astype(jnp.bfloat16)
    for i in range(NORM_PARTS):
        copies[i].wait()
        at = slice(i * part, (i + 1) * part)
        x = x_ref[at, :].astype(jnp.float32)
        meansq = jnp.mean(x * x, axis=-1, keepdims=True)
        out_ref[at, :] = (x * lax.rsqrt(meansq + EPS) * (1.0 / width**0.5)).astype(jnp.bfloat16)


def dot_t(a, b):
    return lax.dot_general(a, b, (((1,), (1,)), ((), ())), preferred_element_type=jnp.float32)


def key_bias(flags):
    ones = jnp.ones((flags.shape[0], 128), jnp.bfloat16)
    return lax.dot_general(flags, ones, (((0,), (0,)), ((), ())), preferred_element_type=jnp.float32)


def fold_rows(s):
    n, w = s.shape
    return jnp.max(s.reshape(n // 8, 8, w), axis=0)


def unit_work(tab, at, stack, biases, acc):
    half = stack.shape[1] // 2
    k, q, h = tab[at], tab[at + 1], tab[at + 2]
    s = dot_t(stack[k], stack[q, pl.ds(pl.multiple_of(h * half, half), half), :])
    s = s + jnp.tile(biases[k], (1, half // 128))
    acc[q, h] = jnp.maximum(acc[q, h], fold_rows(s))


def self_kernel(t_ref, tab, stack, biases, acc, turn):
    rows = stack.shape[1]
    half = rows // 2
    stack[0] = t_ref[:rows, :]
    biases[0] = key_bias(t_ref[rows:, :rows])
    acc[...] = jnp.full(acc.shape, -1.0, jnp.float32)
    for h in range(2):
        n = half * (h + 1)
        s = dot_t(t_ref[:n, :], t_ref[h * half : (h + 1) * half, :])
        key = lax.broadcasted_iota(jnp.int32, (n, half), 0)
        query = lax.broadcasted_iota(jnp.int32, (n, half), 1) + h * half
        s = jnp.where(key < query, s + jnp.tile(biases[0, :n], (1, half // 128)), -1.0)
        acc[0, h] = jnp.maximum(acc[0, h], fold_rows(s))
    turn[...] = jnp.full(turn.shape, tab[0], jnp.int32)


def pair_kernel(tab, turn_in, *refs, new, start, steps, unroll, last):
    n = len(new)
    tiles = refs[:n]
    n_out = 3 * last
    stack, biases, acc = refs[n + 3 : n + 6]
    turn = refs[n + 6]
    outs = refs[n + 7 : n + 7 + n_out]
    sems = refs[n + 7 + n_out]
    rows = stack.shape[1]
    half = rows // 2
    copies = []
    for i, slot in enumerate(new):
        copies.append(pltpu.make_async_copy(tiles[i].at[pl.ds(0, rows)], stack.at[slot], sems.at[i]))
    for c in copies:
        c.start()
    flags = jnp.concatenate([t[rows:, :rows] for t in tiles], axis=0)
    shape = (n * FLAG_ROWS, n * 128)
    row, lane = (lax.broadcasted_iota(jnp.int32, shape, a) for a in range(2))
    spread = (row == lane // 128 * FLAG_ROWS).astype(jnp.bfloat16)
    columns = lax.dot_general(flags, spread, (((0,), (0,)), ((), ())), preferred_element_type=jnp.float32)
    for i, slot in enumerate(new):
        biases[slot] = columns[:, i * 128 : (i + 1) * 128]
    for c in copies:
        c.wait()

    def step(u, carry):
        for j in range(unroll):
            unit_work(tab, len(OFFSETS) + 3 * (start + u * unroll + j), stack, biases, acc)
        return carry

    lax.fori_loop(0, steps, step, 0)
    turn[...] = turn_in[...]
    if last:
        for out in outs:
            out[...] = jnp.full(out.shape, -1.0, jnp.float32)
        for s, (z, y, x) in enumerate(OFFSETS):
            row = 3 * (y % 3 + y // 3 * 2) + x % 3 + x // 3 * 2
            for h in range(2):
                outs[z % 3 + z // 3 * 2][row : row + 1, h * half : (h + 1) * half] = jnp.max(
                    acc[s, h], axis=0, keepdims=True
                )


def on_device(embeddings, row_mask, tile_counts):
    rows, width = embeddings.shape[2:]
    half = rows // 2
    clus, place = lax.axis_index("clus"), lax.axis_index("help")
    table, loops = work_table()
    tab = jnp.asarray(table)[clus, place]
    alive = (place < tile_counts).astype(jnp.int32)
    slots = len(OFFSETS)
    vmem, smem, hbm = (pl.BlockSpec(memory_space=m) for m in (pltpu.VMEM, pltpu.SMEM, pltpu.HBM))
    state = [
        pltpu.VMEM((slots, rows, width), jnp.bfloat16),
        pltpu.VMEM((slots, rows, 128), jnp.float32),
        pltpu.VMEM((slots, 2, 8, half), jnp.float32),
    ]

    own = pl.pallas_call(
        unit_kernel,
        out_shape=pltpu.VMEM((rows + FLAG_ROWS, width), jnp.bfloat16),
        in_specs=[smem, hbm, hbm],
        out_specs=vmem,
        scratch_shapes=[
            pltpu.VMEM((rows, width), jnp.bfloat16),
            pltpu.VMEM((1, rows), jnp.int32),
            pltpu.SemaphoreType.DMA((NORM_PARTS + 1,)),
        ],
        compiler_params=pltpu.CompilerParams(vmem_limit_bytes=56 * 2**20),
    )(alive, embeddings[0, 0], row_mask[0])
    *held_state, turn = pl.pallas_call(
        self_kernel,
        out_shape=state + [jax.ShapeDtypeStruct((8, 128), jnp.int32)],
        in_specs=[vmem, smem],
        out_specs=[vmem] * 4,
        compiler_params=pltpu.CompilerParams(vmem_limit_bytes=24 * 2**20),
        cost_estimate=pl.CostEstimate(flops=1000, bytes_accessed=1000, transcendentals=0),
    )(own, tab)
    held = {OFFSETS[0]: own}
    turns = [turn]
    start, arrived = 0, 0
    for d, source in PLAN:
        if d in GATES:
            held[source], turns[GATES[d]] = lax.optimization_barrier((held[source], turns[GATES[d]]))
        sent = held[source]
        if d in AFTER:
            sent, held[AFTER[d]] = lax.optimization_barrier((sent, held[AFTER[d]]))
        held[d] = lax.ppermute(sent, ("clus", "help"), moves(sub(d, source)))
        i = len(turns) - 1
        if len(held) - 1 < STAGES[i]:
            continue
        steps, unroll = loops[i]
        new = list(range(arrived + 1, STAGES[i] + 1))
        last = i == len(loops) - 1
        outs = [jax.ShapeDtypeStruct((8, 128), jnp.int32)]
        outs += [jax.ShapeDtypeStruct((9, rows), jnp.float32)] * (3 * last)
        results = pl.pallas_call(
            functools.partial(pair_kernel, new=new, start=start, steps=steps, unroll=unroll, last=last),
            out_shape=state + outs,
            in_specs=[smem] + [vmem] * (len(new) + 4),
            out_specs=[vmem] * (3 + len(outs)),
            input_output_aliases={2 + len(new) + j: j for j in range(3)},
            scratch_shapes=[pltpu.SemaphoreType.DMA((len(new),))],
            compiler_params=pltpu.CompilerParams(vmem_limit_bytes=24 * 2**20),
            cost_estimate=pl.CostEstimate(flops=1000, bytes_accessed=1000, transcendentals=0),
        )(tab, turns[i], *[held[OFFSETS[s]] for s in new], *held_state)
        held_state, finals = results[:3], results[4:]
        turns.append(results[3])
        start += steps * unroll
        arrived = STAGES[i]
    own_part, ahead, behind = finals
    for axis in range(3):
        step = [0, 0, 0]
        step[axis] = 1
        back = [0, 0, 0]
        back[axis] = 3
        ahead = lax.ppermute(ahead, ("clus", "help"), moves(back))
        behind = lax.ppermute(behind, ("clus", "help"), moves(step))
        merged = jnp.maximum(own_part, jnp.maximum(ahead, behind))
        n = merged.shape[0] // 3
        if axis < 2:
            own_part, ahead, behind = merged[:n], merged[n : 2 * n], merged[2 * n :]
    return merged[None]


def solution(mesh):
    in_specs = (P("clus", "help", None, None), P("clus", "help", None), P("clus"))
    out_specs = P("clus", "help", None)
    return jax.shard_map(on_device, mesh=mesh, in_specs=in_specs, out_specs=out_specs, check_vma=False)
```

```python
import functools

import jax
import jax.numpy as jnp
import numpy as np
from jax import lax
from jax.experimental import pallas as pl
from jax.experimental.pallas import tpu as pltpu
from jax.sharding import PartitionSpec as P

EPS = 1e-06
SIDE = 4
UNROLL = 12
FLAG_ROWS = 16
DEAD = -4.0
NORM_PARTS = 2

PLAN = [
    ((0, 0, 1), (0, 0, 0)),
    ((3, 1, 0), (0, 0, 0)),
    ((0, 3, 1), (0, 0, 1)),
    ((3, 0, 3), (0, 0, 0)),
    ((1, 0, 0), (0, 0, 0)),
    ((3, 1, 3), (3, 1, 0)),
    ((3, 1, 1), (3, 1, 0)),
    ((1, 3, 1), (0, 3, 1)),
    ((3, 3, 3), (3, 0, 3)),
    ((1, 1, 0), (1, 0, 0)),
]
OFFSETS = [(0, 0, 0)] + [d for d, _ in PLAN]
STAGES = [2, 4, 7, 9, 10]
GATES = {(0, 3, 1): 0, (1, 3, 1): 1, (1, 1, 0): 2}
AFTER = {(1, 0, 0): (0, 0, 1), (3, 0, 3): (0, 0, 1)}


def turned(d):
    return (-d[0], -d[2], -d[1])


def place_of(v):
    return ((v[0] % SIDE) * SIDE + v[1] % SIDE) * SIDE + v[2] % SIDE


def cube():
    return [(z, y, x) for z in range(SIDE) for y in range(SIDE) for x in range(SIDE)]


def add(a, b):
    return tuple(x + y for x, y in zip(a, b))


def sub(a, b):
    return tuple((x - y) % SIDE for x, y in zip(a, b))


def moves(step):
    pairs = []
    for c in range(2):
        s = turned(step) if c else step
        for v in cube():
            pairs.append((c * SIDE**3 + place_of(add(v, s)), c * SIDE**3 + place_of(v)))
    return pairs


def choose_pairs():
    best = {}
    for a in range(len(OFFSETS)):
        for b in range(a):
            g = sub(OFFSETS[a], OFFSETS[b])
            key = min(g, sub((0, 0, 0), g))
            if key not in best:
                best[key] = (a, b)
    assert len(best) == (SIDE**3 - 1 + 7) // 2
    return sorted(best.values())


def work_table():
    full, halved = [[] for _ in STAGES], [[] for _ in STAGES]
    for a, b in choose_pairs():
        stage = next(i for i, n in enumerate(STAGES) if a <= n)
        twin = all((2 * g) % SIDE == 0 for g in sub(OFFSETS[a], OFFSETS[b]))
        (halved if twin else full)[stage].append((a, b))
    loops, units = [], []
    for f, h in zip(full, halved):
        steps = -(-len(f) // UNROLL)
        unroll = -(-len(f) // max(steps, 1))
        f = f + f[-1:] * (steps * unroll - len(f))
        loops.append((steps, unroll, len(h)))
        units += f + h
    table = np.zeros((2, SIDE**3, len(units) * 3), np.int32)
    for c in range(2):
        offs = [turned(d) if c else d for d in OFFSETS]
        for v in cube():
            for n, (a, b) in enumerate(units):
                first = place_of(add(v, offs[a])) < place_of(add(v, offs[b]))
                k, q = (a, b) if first else (b, a)
                table[c, place_of(v), 3 * n : 3 * n + 3] = (k, q, int(first))
    return table, loops


def unit_kernel(alive, x_hbm, mask_hbm, out_ref, x_ref, mask_ref, sems):
    rows, width = x_ref.shape
    part = rows // NORM_PARTS
    copies = []
    for i in range(NORM_PARTS):
        at = pl.ds(i * part, part)
        copies.append(pltpu.make_async_copy(x_hbm.at[at], x_ref.at[at], sems.at[i]))
        copies[-1].start()
    copies.append(pltpu.make_async_copy(mask_hbm, mask_ref, sems.at[NORM_PARTS]))
    copies[-1].start()
    copies[-1].wait()
    live = (mask_ref[...] == 1) & (alive[0] == 1)
    bias = jnp.broadcast_to(jnp.where(live, 0.0, DEAD), (FLAG_ROWS, rows))
    top = lax.broadcasted_iota(jnp.int32, (FLAG_ROWS, rows), 0) == 0
    out_ref[rows:, :] = jnp.zeros((FLAG_ROWS, width), jnp.bfloat16)
    out_ref[rows:, :rows] = jnp.where(top, bias, 0.0).astype(jnp.bfloat16)
    for i in range(NORM_PARTS):
        copies[i].wait()
        at = slice(i * part, (i + 1) * part)
        x = x_ref[at, :].astype(jnp.float32)
        meansq = jnp.mean(x * x, axis=-1, keepdims=True)
        out_ref[at, :] = (x * lax.rsqrt(meansq + EPS) * (1.0 / width**0.5)).astype(jnp.bfloat16)


def dot_t(a, b):
    return lax.dot_general(a, b, (((1,), (1,)), ((), ())), preferred_element_type=jnp.float32)


def key_bias(flags):
    ones = jnp.ones((flags.shape[0], 128), jnp.bfloat16)
    return lax.dot_general(flags, ones, (((0,), (0,)), ((), ())), preferred_element_type=jnp.float32)


def fold_rows(s):
    n, w = s.shape
    return jnp.max(s.reshape(n // 8, 8, w), axis=0)


def pair_work(tab, at, stack, biases, acc, halved):
    rows = stack.shape[1]
    half = rows // 2
    k, q, h = tab[at], tab[at + 1], tab[at + 2]
    query = stack[q, pl.ds(pl.multiple_of(h * half, half), half), :] if halved else stack[q]
    s = dot_t(stack[k], query)
    s = fold_rows(s + jnp.tile(biases[k], (1, s.shape[1] // 128)))
    if halved:
        acc[q, h] = jnp.maximum(acc[q, h], s)
    else:
        for i in range(2):
            acc[q, i] = jnp.maximum(acc[q, i], s[:, i * half : (i + 1) * half])


def self_kernel(t_ref, tab, stack, biases, acc, turn):
    rows = stack.shape[1]
    half = rows // 2
    stack[0] = t_ref[:rows, :]
    biases[0] = key_bias(t_ref[rows:, :rows])
    acc[...] = jnp.full(acc.shape, -1.0, jnp.float32)
    for h in range(2):
        n = half * (h + 1)
        s = dot_t(t_ref[:n, :], t_ref[h * half : (h + 1) * half, :])
        key = lax.broadcasted_iota(jnp.int32, (n, half), 0)
        query = lax.broadcasted_iota(jnp.int32, (n, half), 1) + h * half
        s = jnp.where(key < query, s + jnp.tile(biases[0, :n], (1, half // 128)), -1.0)
        acc[0, h] = jnp.maximum(acc[0, h], fold_rows(s))
    turn[...] = jnp.full(turn.shape, tab[0], jnp.int32)


def pair_kernel(tab, turn_in, *refs, new, start, steps, unroll, halved, last):
    n = len(new)
    tiles = refs[:n]
    n_out = 3 * last
    stack, biases, acc = refs[n + 3 : n + 6]
    turn = refs[n + 6]
    outs = refs[n + 7 : n + 7 + n_out]
    rows = stack.shape[1]
    half = rows // 2
    flags = jnp.concatenate([t[rows:, :rows] for t in tiles], axis=0)
    shape = (n * FLAG_ROWS, n * 128)
    row, lane = (lax.broadcasted_iota(jnp.int32, shape, a) for a in range(2))
    spread = (row == lane // 128 * FLAG_ROWS).astype(jnp.bfloat16)
    columns = lax.dot_general(flags, spread, (((0,), (0,)), ((), ())), preferred_element_type=jnp.float32)
    for i, slot in enumerate(new):
        biases[slot] = columns[:, i * 128 : (i + 1) * 128]
    for i, slot in enumerate(new):
        stack[slot] = tiles[i][:rows, :]

    def step(u, carry):
        for j in range(unroll):
            pair_work(tab, 3 * (start + u * unroll + j), stack, biases, acc, False)
        return carry

    lax.fori_loop(0, steps, step, 0)
    for j in range(halved):
        pair_work(tab, 3 * (start + steps * unroll + j), stack, biases, acc, True)
    turn[...] = turn_in[...]
    if last:
        for out in outs:
            out[...] = jnp.full(out.shape, -1.0, jnp.float32)
        for s, (z, y, x) in enumerate(OFFSETS):
            row = 3 * (y % 3 + y // 3 * 2) + x % 3 + x // 3 * 2
            for h in range(2):
                outs[z % 3 + z // 3 * 2][row : row + 1, h * half : (h + 1) * half] = jnp.max(
                    acc[s, h], axis=0, keepdims=True
                )


def on_device(embeddings, row_mask, tile_counts):
    rows, width = embeddings.shape[2:]
    half = rows // 2
    clus, place = lax.axis_index("clus"), lax.axis_index("help")
    table, loops = work_table()
    tab = jnp.asarray(table)[clus, place]
    alive = (place < tile_counts).astype(jnp.int32)
    slots = len(OFFSETS)
    vmem, smem, hbm = (pl.BlockSpec(memory_space=m) for m in (pltpu.VMEM, pltpu.SMEM, pltpu.HBM))
    state = [
        pltpu.VMEM((slots, rows, width), jnp.bfloat16),
        pltpu.VMEM((slots, rows, 128), jnp.float32),
        pltpu.VMEM((slots, 2, 8, half), jnp.float32),
    ]

    own = pl.pallas_call(
        unit_kernel,
        out_shape=pltpu.VMEM((rows + FLAG_ROWS, width), jnp.bfloat16),
        in_specs=[smem, hbm, hbm],
        out_specs=vmem,
        scratch_shapes=[
            pltpu.VMEM((rows, width), jnp.bfloat16),
            pltpu.VMEM((1, rows), jnp.int32),
            pltpu.SemaphoreType.DMA((NORM_PARTS + 1,)),
        ],
        compiler_params=pltpu.CompilerParams(vmem_limit_bytes=56 * 2**20),
    )(alive, embeddings[0, 0], row_mask[0])
    *held_state, turn = pl.pallas_call(
        self_kernel,
        out_shape=state + [jax.ShapeDtypeStruct((8, 128), jnp.int32)],
        in_specs=[vmem, smem],
        out_specs=[vmem] * 4,
        compiler_params=pltpu.CompilerParams(vmem_limit_bytes=24 * 2**20),
        cost_estimate=pl.CostEstimate(flops=1000, bytes_accessed=1000, transcendentals=0),
    )(own, tab)
    held = {OFFSETS[0]: own}
    turns = [turn]
    start, arrived = 0, 0
    for d, source in PLAN:
        if d in GATES:
            held[source], turns[GATES[d]] = lax.optimization_barrier((held[source], turns[GATES[d]]))
        sent = held[source]
        if d in AFTER:
            sent, held[AFTER[d]] = lax.optimization_barrier((sent, held[AFTER[d]]))
        held[d] = lax.ppermute(sent, ("clus", "help"), moves(sub(d, source)))
        i = len(turns) - 1
        if len(held) - 1 < STAGES[i]:
            continue
        steps, unroll, halved = loops[i]
        new = list(range(arrived + 1, STAGES[i] + 1))
        last = i == len(loops) - 1
        outs = [jax.ShapeDtypeStruct((8, 128), jnp.int32)]
        outs += [jax.ShapeDtypeStruct((9, rows), jnp.float32)] * (3 * last)
        results = pl.pallas_call(
            functools.partial(pair_kernel, new=new, start=start, steps=steps, unroll=unroll, halved=halved, last=last),
            out_shape=state + outs,
            in_specs=[smem] + [vmem] * (len(new) + 4),
            out_specs=[vmem] * (3 + len(outs)),
            input_output_aliases={2 + len(new) + j: j for j in range(3)},
            compiler_params=pltpu.CompilerParams(vmem_limit_bytes=24 * 2**20),
            cost_estimate=pl.CostEstimate(flops=1000, bytes_accessed=1000, transcendentals=0),
        )(tab, turns[i], *[held[OFFSETS[s]] for s in new], *held_state)
        held_state, finals = results[:3], results[4:]
        turns.append(results[3])
        start += steps * unroll + halved
        arrived = STAGES[i]
    own_part, ahead, behind = finals
    for axis in range(3):
        step = [0, 0, 0]
        step[axis] = 1
        back = [0, 0, 0]
        back[axis] = 3
        ahead = lax.ppermute(ahead, ("clus", "help"), moves(back))
        behind = lax.ppermute(behind, ("clus", "help"), moves(step))
        merged = jnp.maximum(own_part, jnp.maximum(ahead, behind))
        n = merged.shape[0] // 3
        if axis < 2:
            own_part, ahead, behind = merged[:n], merged[n : 2 * n], merged[2 * n :]
    return merged[None]


def solution(mesh):
    in_specs = (P("clus", "help", None, None), P("clus", "help", None), P("clus"))
    out_specs = P("clus", "help", None)
    return jax.shard_map(on_device, mesh=mesh, in_specs=in_specs, out_specs=out_specs, check_vma=False)
```

```python
import functools

import jax
import jax.numpy as jnp
import numpy as np
from jax import lax
from jax.experimental import pallas as pl
from jax.experimental.pallas import tpu as pltpu
from jax.sharding import PartitionSpec as P

EPS = 1e-06
SIDE = 4
UNROLL = 12
FLAG_ROWS = 16
DEAD = -4.0
NORM_PARTS = 2

PLAN = [
    ((0, 1, 0), (0, 0, 0)),
    ((3, 0, 1), (0, 0, 0)),
    ((0, 1, 3), (0, 1, 0)),
    ((3, 3, 0), (0, 0, 0)),
    ((1, 0, 0), (0, 0, 0)),
    ((3, 3, 1), (3, 0, 1)),
    ((3, 1, 1), (3, 0, 1)),
    ((1, 1, 3), (0, 1, 3)),
    ((3, 3, 3), (3, 3, 0)),
    ((1, 0, 1), (1, 0, 0)),
]
OFFSETS = [(0, 0, 0)] + [d for d, _ in PLAN]
STAGES = [2, 4, 5, 7, 9, 10]
GATES = {(0, 1, 3): 0, (1, 1, 3): 1, (1, 0, 1): 2}
AFTER = {(1, 0, 0): (0, 1, 0), (3, 3, 0): (0, 1, 0)}


def turned(d):
    return (-d[0], -d[2], -d[1])


def place_of(v):
    return ((v[0] % SIDE) * SIDE + v[1] % SIDE) * SIDE + v[2] % SIDE


def cube():
    return [(z, y, x) for z in range(SIDE) for y in range(SIDE) for x in range(SIDE)]


def add(a, b):
    return tuple(x + y for x, y in zip(a, b))


def sub(a, b):
    return tuple((x - y) % SIDE for x, y in zip(a, b))


def moves(step):
    pairs = []
    for c in range(2):
        s = turned(step) if c else step
        for v in cube():
            pairs.append((c * SIDE**3 + place_of(add(v, s)), c * SIDE**3 + place_of(v)))
    return pairs


def choose_pairs():
    best = {}
    for a in range(len(OFFSETS)):
        for b in range(a):
            g = sub(OFFSETS[a], OFFSETS[b])
            key = min(g, sub((0, 0, 0), g))
            if key not in best:
                best[key] = (a, b)
    assert len(best) == (SIDE**3 - 1 + 7) // 2
    return sorted(best.values())


def work_table():
    full, halved = [[] for _ in STAGES], [[] for _ in STAGES]
    for a, b in choose_pairs():
        stage = next(i for i, n in enumerate(STAGES) if a <= n)
        twin = all((2 * g) % SIDE == 0 for g in sub(OFFSETS[a], OFFSETS[b]))
        (halved if twin else full)[stage].append((a, b))
    loops, units = [], []
    for f, h in zip(full, halved):
        steps = -(-len(f) // UNROLL)
        unroll = -(-len(f) // max(steps, 1))
        f = f + f[-1:] * (steps * unroll - len(f))
        loops.append((steps, unroll, len(h)))
        units += f + h
    table = np.zeros((2, SIDE**3, len(units) * 3), np.int32)
    for c in range(2):
        offs = [turned(d) if c else d for d in OFFSETS]
        for v in cube():
            for n, (a, b) in enumerate(units):
                first = place_of(add(v, offs[a])) < place_of(add(v, offs[b]))
                k, q = (a, b) if first else (b, a)
                table[c, place_of(v), 3 * n : 3 * n + 3] = (k, q, int(first))
    return table, loops


def unit_kernel(alive, x_hbm, mask_hbm, out_ref, x_ref, mask_ref, sems):
    rows, width = x_ref.shape
    part = rows // NORM_PARTS
    copies = []
    for i in range(NORM_PARTS):
        at = pl.ds(i * part, part)
        copies.append(pltpu.make_async_copy(x_hbm.at[at], x_ref.at[at], sems.at[i]))
        copies[-1].start()
    copies.append(pltpu.make_async_copy(mask_hbm, mask_ref, sems.at[NORM_PARTS]))
    copies[-1].start()
    copies[-1].wait()
    live = (mask_ref[...] == 1) & (alive[0] == 1)
    bias = jnp.broadcast_to(jnp.where(live, 0.0, DEAD), (FLAG_ROWS, rows))
    top = lax.broadcasted_iota(jnp.int32, (FLAG_ROWS, rows), 0) == 0
    out_ref[rows:, :] = jnp.zeros((FLAG_ROWS, width), jnp.bfloat16)
    out_ref[rows:, :rows] = jnp.where(top, bias, 0.0).astype(jnp.bfloat16)
    for i in range(NORM_PARTS):
        copies[i].wait()
        at = slice(i * part, (i + 1) * part)
        x = x_ref[at, :].astype(jnp.float32)
        meansq = jnp.mean(x * x, axis=-1, keepdims=True)
        out_ref[at, :] = (x * lax.rsqrt(meansq + EPS) * (1.0 / width**0.5)).astype(jnp.bfloat16)


def dot_t(a, b):
    return lax.dot_general(a, b, (((1,), (1,)), ((), ())), preferred_element_type=jnp.float32)


def key_bias(flags):
    ones = jnp.ones((flags.shape[0], 128), jnp.bfloat16)
    return lax.dot_general(flags, ones, (((0,), (0,)), ((), ())), preferred_element_type=jnp.float32)


def fold_rows(s):
    n, w = s.shape
    return jnp.max(s.reshape(n // 8, 8, w), axis=0)


def pair_work(tab, at, stack, biases, acc, halved):
    rows = stack.shape[1]
    half = rows // 2
    k, q, h = tab[at], tab[at + 1], tab[at + 2]
    query = stack[q, pl.ds(pl.multiple_of(h * half, half), half), :] if halved else stack[q]
    s = dot_t(stack[k], query)
    s = fold_rows(s + jnp.tile(biases[k], (1, s.shape[1] // 128)))
    if halved:
        acc[q, h] = jnp.maximum(acc[q, h], s)
    else:
        for i in range(2):
            acc[q, i] = jnp.maximum(acc[q, i], s[:, i * half : (i + 1) * half])


def self_kernel(t_ref, tab, stack, biases, acc, turn):
    rows = stack.shape[1]
    half = rows // 2
    stack[0] = t_ref[:rows, :]
    biases[0] = key_bias(t_ref[rows:, :rows])
    acc[...] = jnp.full(acc.shape, -1.0, jnp.float32)
    for h in range(2):
        n = half * (h + 1)
        s = dot_t(t_ref[:n, :], t_ref[h * half : (h + 1) * half, :])
        key = lax.broadcasted_iota(jnp.int32, (n, half), 0)
        query = lax.broadcasted_iota(jnp.int32, (n, half), 1) + h * half
        s = jnp.where(key < query, s + jnp.tile(biases[0, :n], (1, half // 128)), -1.0)
        acc[0, h] = jnp.maximum(acc[0, h], fold_rows(s))
    turn[...] = jnp.full(turn.shape, tab[0], jnp.int32)


def pair_kernel(tab, turn_in, *refs, new, start, steps, unroll, halved, last):
    n = len(new)
    tiles = refs[:n]
    n_out = 3 * last
    stack, biases, acc = refs[n + 3 : n + 6]
    turn = refs[n + 6]
    outs = refs[n + 7 : n + 7 + n_out]
    rows = stack.shape[1]
    half = rows // 2
    flags = jnp.concatenate([t[rows:, :rows] for t in tiles], axis=0)
    shape = (n * FLAG_ROWS, n * 128)
    row, lane = (lax.broadcasted_iota(jnp.int32, shape, a) for a in range(2))
    spread = (row == lane // 128 * FLAG_ROWS).astype(jnp.bfloat16)
    columns = lax.dot_general(flags, spread, (((0,), (0,)), ((), ())), preferred_element_type=jnp.float32)
    for i, slot in enumerate(new):
        biases[slot] = columns[:, i * 128 : (i + 1) * 128]
    for i, slot in enumerate(new):
        stack[slot] = tiles[i][:rows, :]

    def step(u, carry):
        for j in range(unroll):
            pair_work(tab, 3 * (start + u * unroll + j), stack, biases, acc, False)
        return carry

    lax.fori_loop(0, steps, step, 0)
    for j in range(halved):
        pair_work(tab, 3 * (start + steps * unroll + j), stack, biases, acc, True)
    turn[...] = turn_in[...]
    if last:
        for out in outs:
            out[...] = jnp.full(out.shape, -1.0, jnp.float32)
        for s, (z, y, x) in enumerate(OFFSETS):
            row = 3 * (y % 3 + y // 3 * 2) + x % 3 + x // 3 * 2
            for h in range(2):
                outs[z % 3 + z // 3 * 2][row : row + 1, h * half : (h + 1) * half] = jnp.max(
                    acc[s, h], axis=0, keepdims=True
                )


def on_device(embeddings, row_mask, tile_counts):
    rows, width = embeddings.shape[2:]
    half = rows // 2
    clus, place = lax.axis_index("clus"), lax.axis_index("help")
    table, loops = work_table()
    tab = jnp.asarray(table)[clus, place]
    alive = (place < tile_counts).astype(jnp.int32)
    slots = len(OFFSETS)
    vmem, smem, hbm = (pl.BlockSpec(memory_space=m) for m in (pltpu.VMEM, pltpu.SMEM, pltpu.HBM))
    state = [
        pltpu.VMEM((slots, rows, width), jnp.bfloat16),
        pltpu.VMEM((slots, rows, 128), jnp.float32),
        pltpu.VMEM((slots, 2, 8, half), jnp.float32),
    ]

    own = pl.pallas_call(
        unit_kernel,
        out_shape=pltpu.VMEM((rows + FLAG_ROWS, width), jnp.bfloat16),
        in_specs=[smem, hbm, hbm],
        out_specs=vmem,
        scratch_shapes=[
            pltpu.VMEM((rows, width), jnp.bfloat16),
            pltpu.VMEM((1, rows), jnp.int32),
            pltpu.SemaphoreType.DMA((NORM_PARTS + 1,)),
        ],
        compiler_params=pltpu.CompilerParams(vmem_limit_bytes=56 * 2**20),
    )(alive, embeddings[0, 0], row_mask[0])
    *held_state, turn = pl.pallas_call(
        self_kernel,
        out_shape=state + [jax.ShapeDtypeStruct((8, 128), jnp.int32)],
        in_specs=[vmem, smem],
        out_specs=[vmem] * 4,
        compiler_params=pltpu.CompilerParams(vmem_limit_bytes=24 * 2**20),
        cost_estimate=pl.CostEstimate(flops=1000, bytes_accessed=1000, transcendentals=0),
    )(own, tab)
    held = {OFFSETS[0]: own}
    turns = [turn]
    start, arrived = 0, 0
    for d, source in PLAN:
        if d in GATES:
            held[source], turns[GATES[d]] = lax.optimization_barrier((held[source], turns[GATES[d]]))
        sent = held[source]
        if d in AFTER:
            sent, held[AFTER[d]] = lax.optimization_barrier((sent, held[AFTER[d]]))
        held[d] = lax.ppermute(sent, ("clus", "help"), moves(sub(d, source)))
        i = len(turns) - 1
        if len(held) - 1 < STAGES[i]:
            continue
        steps, unroll, halved = loops[i]
        new = list(range(arrived + 1, STAGES[i] + 1))
        last = i == len(loops) - 1
        outs = [jax.ShapeDtypeStruct((8, 128), jnp.int32)]
        outs += [jax.ShapeDtypeStruct((9, rows), jnp.float32)] * (3 * last)
        results = pl.pallas_call(
            functools.partial(pair_kernel, new=new, start=start, steps=steps, unroll=unroll, halved=halved, last=last),
            out_shape=state + outs,
            in_specs=[smem] + [vmem] * (len(new) + 4),
            out_specs=[vmem] * (3 + len(outs)),
            input_output_aliases={2 + len(new) + j: j for j in range(3)},
            compiler_params=pltpu.CompilerParams(vmem_limit_bytes=24 * 2**20),
            cost_estimate=pl.CostEstimate(flops=1000, bytes_accessed=1000, transcendentals=0),
        )(tab, turns[i], *[held[OFFSETS[s]] for s in new], *held_state)
        held_state, finals = results[:3], results[4:]
        turns.append(results[3])
        start += steps * unroll + halved
        arrived = STAGES[i]
    own_part, ahead, behind = finals
    for axis in range(3):
        step = [0, 0, 0]
        step[axis] = 1
        back = [0, 0, 0]
        back[axis] = 3
        ahead = lax.ppermute(ahead, ("clus", "help"), moves(back))
        behind = lax.ppermute(behind, ("clus", "help"), moves(step))
        merged = jnp.maximum(own_part, jnp.maximum(ahead, behind))
        n = merged.shape[0] // 3
        if axis < 2:
            own_part, ahead, behind = merged[:n], merged[n : 2 * n], merged[2 * n :]
    return merged[None]


def solution(mesh):
    in_specs = (P("clus", "help", None, None), P("clus", "help", None), P("clus"))
    out_specs = P("clus", "help", None)
    return jax.shard_map(on_device, mesh=mesh, in_specs=in_specs, out_specs=out_specs, check_vma=False)
```

```python
import functools

import jax
import jax.numpy as jnp
import numpy as np
from jax import lax
from jax.experimental import pallas as pl
from jax.experimental.pallas import tpu as pltpu
from jax.sharding import PartitionSpec as P

EPS = 1e-06
SIDE = 4
UNROLL = 12
FLAG_ROWS = 16
DEAD = -4.0
NORM_PARTS = 2

PLAN = [
    ((0, 1, 0), (0, 0, 0)),
    ((3, 0, 1), (0, 0, 0)),
    ((0, 1, 3), (0, 1, 0)),
    ((3, 3, 0), (0, 0, 0)),
    ((1, 0, 0), (0, 0, 0)),
    ((3, 3, 1), (3, 0, 1)),
    ((3, 1, 1), (3, 0, 1)),
    ((1, 1, 3), (0, 1, 3)),
    ((3, 3, 3), (3, 3, 0)),
    ((1, 0, 1), (1, 0, 0)),
]
OFFSETS = [(0, 0, 0)] + [d for d, _ in PLAN]
STAGES = [2, 3, 4, 5, 7, 9, 10]
GATES = {(0, 1, 3): 0, (1, 1, 3): 1, (1, 0, 1): 3}
AFTER = {(1, 0, 0): (0, 1, 0), (3, 3, 0): (0, 1, 0)}


def turned(d):
    return (-d[0], -d[2], -d[1])


def place_of(v):
    return ((v[0] % SIDE) * SIDE + v[1] % SIDE) * SIDE + v[2] % SIDE


def cube():
    return [(z, y, x) for z in range(SIDE) for y in range(SIDE) for x in range(SIDE)]


def add(a, b):
    return tuple(x + y for x, y in zip(a, b))


def sub(a, b):
    return tuple((x - y) % SIDE for x, y in zip(a, b))


def moves(step):
    pairs = []
    for c in range(2):
        s = turned(step) if c else step
        for v in cube():
            pairs.append((c * SIDE**3 + place_of(add(v, s)), c * SIDE**3 + place_of(v)))
    return pairs


def choose_pairs():
    best = {}
    for a in range(len(OFFSETS)):
        for b in range(a):
            g = sub(OFFSETS[a], OFFSETS[b])
            key = min(g, sub((0, 0, 0), g))
            if key not in best:
                best[key] = (a, b)
    assert len(best) == (SIDE**3 - 1 + 7) // 2
    return sorted(best.values())


def work_table():
    full, halved = [[] for _ in STAGES], [[] for _ in STAGES]
    for a, b in choose_pairs():
        stage = next(i for i, n in enumerate(STAGES) if a <= n)
        twin = all((2 * g) % SIDE == 0 for g in sub(OFFSETS[a], OFFSETS[b]))
        (halved if twin else full)[stage].append((a, b))
    loops, units = [], []
    for f, h in zip(full, halved):
        steps = -(-len(f) // UNROLL)
        unroll = -(-len(f) // max(steps, 1))
        f = f + f[-1:] * (steps * unroll - len(f))
        loops.append((steps, unroll, len(h)))
        units += f + h
    table = np.zeros((2, SIDE**3, len(units) * 3), np.int32)
    for c in range(2):
        offs = [turned(d) if c else d for d in OFFSETS]
        for v in cube():
            for n, (a, b) in enumerate(units):
                first = place_of(add(v, offs[a])) < place_of(add(v, offs[b]))
                k, q = (a, b) if first else (b, a)
                table[c, place_of(v), 3 * n : 3 * n + 3] = (k, q, int(first))
    return table, loops


def unit_kernel(alive, x_hbm, mask_hbm, out_ref, x_ref, mask_ref, sems):
    rows, width = x_ref.shape
    part = rows // NORM_PARTS
    copies = []
    for i in range(NORM_PARTS):
        at = pl.ds(i * part, part)
        copies.append(pltpu.make_async_copy(x_hbm.at[at], x_ref.at[at], sems.at[i]))
        copies[-1].start()
    copies.append(pltpu.make_async_copy(mask_hbm, mask_ref, sems.at[NORM_PARTS]))
    copies[-1].start()
    copies[-1].wait()
    live = (mask_ref[...] == 1) & (alive[0] == 1)
    bias = jnp.broadcast_to(jnp.where(live, 0.0, DEAD), (FLAG_ROWS, rows))
    top = lax.broadcasted_iota(jnp.int32, (FLAG_ROWS, rows), 0) == 0
    out_ref[rows:, :] = jnp.zeros((FLAG_ROWS, width), jnp.bfloat16)
    out_ref[rows:, :rows] = jnp.where(top, bias, 0.0).astype(jnp.bfloat16)
    for i in range(NORM_PARTS):
        copies[i].wait()
        at = slice(i * part, (i + 1) * part)
        x = x_ref[at, :].astype(jnp.float32)
        meansq = jnp.mean(x * x, axis=-1, keepdims=True)
        out_ref[at, :] = (x * lax.rsqrt(meansq + EPS) * (1.0 / width**0.5)).astype(jnp.bfloat16)


def dot_t(a, b):
    return lax.dot_general(a, b, (((1,), (1,)), ((), ())), preferred_element_type=jnp.float32)


def key_bias(flags):
    ones = jnp.ones((flags.shape[0], 128), jnp.bfloat16)
    return lax.dot_general(flags, ones, (((0,), (0,)), ((), ())), preferred_element_type=jnp.float32)


def fold_rows(s):
    n, w = s.shape
    return jnp.max(s.reshape(n // 8, 8, w), axis=0)


def pair_work(tab, at, stack, biases, acc, halved):
    rows = stack.shape[1]
    half = rows // 2
    k, q, h = tab[at], tab[at + 1], tab[at + 2]
    query = stack[q, pl.ds(pl.multiple_of(h * half, half), half), :] if halved else stack[q]
    s = dot_t(stack[k], query)
    s = fold_rows(s + jnp.tile(biases[k], (1, s.shape[1] // 128)))
    if halved:
        acc[q, h] = jnp.maximum(acc[q, h], s)
    else:
        for i in range(2):
            acc[q, i] = jnp.maximum(acc[q, i], s[:, i * half : (i + 1) * half])


def self_kernel(t_ref, tab, stack, biases, acc, turn):
    rows = stack.shape[1]
    half = rows // 2
    stack[0] = t_ref[:rows, :]
    biases[0] = key_bias(t_ref[rows:, :rows])
    acc[...] = jnp.full(acc.shape, -1.0, jnp.float32)
    for h in range(2):
        n = half * (h + 1)
        s = dot_t(t_ref[:n, :], t_ref[h * half : (h + 1) * half, :])
        key = lax.broadcasted_iota(jnp.int32, (n, half), 0)
        query = lax.broadcasted_iota(jnp.int32, (n, half), 1) + h * half
        s = jnp.where(key < query, s + jnp.tile(biases[0, :n], (1, half // 128)), -1.0)
        acc[0, h] = jnp.maximum(acc[0, h], fold_rows(s))
    turn[...] = jnp.full(turn.shape, tab[0], jnp.int32)


def pair_kernel(tab, turn_in, *refs, new, start, steps, unroll, halved, last):
    n = len(new)
    tiles = refs[:n]
    n_out = 3 * last
    stack, biases, acc = refs[n + 3 : n + 6]
    turn = refs[n + 6]
    outs = refs[n + 7 : n + 7 + n_out]
    rows = stack.shape[1]
    half = rows // 2
    flags = jnp.concatenate([t[rows:, :rows] for t in tiles], axis=0)
    shape = (n * FLAG_ROWS, n * 128)
    row, lane = (lax.broadcasted_iota(jnp.int32, shape, a) for a in range(2))
    spread = (row == lane // 128 * FLAG_ROWS).astype(jnp.bfloat16)
    columns = lax.dot_general(flags, spread, (((0,), (0,)), ((), ())), preferred_element_type=jnp.float32)
    for i, slot in enumerate(new):
        biases[slot] = columns[:, i * 128 : (i + 1) * 128]
    for i, slot in enumerate(new):
        stack[slot] = tiles[i][:rows, :]

    def step(u, carry):
        for j in range(unroll):
            pair_work(tab, 3 * (start + u * unroll + j), stack, biases, acc, False)
        return carry

    lax.fori_loop(0, steps, step, 0)
    for j in range(halved):
        pair_work(tab, 3 * (start + steps * unroll + j), stack, biases, acc, True)
    turn[...] = turn_in[...]
    if last:
        for out in outs:
            out[...] = jnp.full(out.shape, -1.0, jnp.float32)
        for s, (z, y, x) in enumerate(OFFSETS):
            row = 3 * (y % 3 + y // 3 * 2) + x % 3 + x // 3 * 2
            for h in range(2):
                outs[z % 3 + z // 3 * 2][row : row + 1, h * half : (h + 1) * half] = jnp.max(
                    acc[s, h], axis=0, keepdims=True
                )


def on_device(embeddings, row_mask, tile_counts):
    rows, width = embeddings.shape[2:]
    half = rows // 2
    clus, place = lax.axis_index("clus"), lax.axis_index("help")
    table, loops = work_table()
    tab = jnp.asarray(table)[clus, place]
    alive = (place < tile_counts).astype(jnp.int32)
    slots = len(OFFSETS)
    vmem, smem, hbm = (pl.BlockSpec(memory_space=m) for m in (pltpu.VMEM, pltpu.SMEM, pltpu.HBM))
    state = [
        pltpu.VMEM((slots, rows, width), jnp.bfloat16),
        pltpu.VMEM((slots, rows, 128), jnp.float32),
        pltpu.VMEM((slots, 2, 8, half), jnp.float32),
    ]

    own = pl.pallas_call(
        unit_kernel,
        out_shape=pltpu.VMEM((rows + FLAG_ROWS, width), jnp.bfloat16),
        in_specs=[smem, hbm, hbm],
        out_specs=vmem,
        scratch_shapes=[
            pltpu.VMEM((rows, width), jnp.bfloat16),
            pltpu.VMEM((1, rows), jnp.int32),
            pltpu.SemaphoreType.DMA((NORM_PARTS + 1,)),
        ],
        compiler_params=pltpu.CompilerParams(vmem_limit_bytes=56 * 2**20),
    )(alive, embeddings[0, 0], row_mask[0])
    *held_state, turn = pl.pallas_call(
        self_kernel,
        out_shape=state + [jax.ShapeDtypeStruct((8, 128), jnp.int32)],
        in_specs=[vmem, smem],
        out_specs=[vmem] * 4,
        compiler_params=pltpu.CompilerParams(vmem_limit_bytes=24 * 2**20),
        cost_estimate=pl.CostEstimate(flops=1000, bytes_accessed=1000, transcendentals=0),
    )(own, tab)
    held = {OFFSETS[0]: own}
    turns = [turn]
    start, arrived = 0, 0
    for d, source in PLAN:
        if d in GATES:
            held[source], turns[GATES[d]] = lax.optimization_barrier((held[source], turns[GATES[d]]))
        sent = held[source]
        if d in AFTER:
            sent, held[AFTER[d]] = lax.optimization_barrier((sent, held[AFTER[d]]))
        held[d] = lax.ppermute(sent, ("clus", "help"), moves(sub(d, source)))
        i = len(turns) - 1
        if len(held) - 1 < STAGES[i]:
            continue
        steps, unroll, halved = loops[i]
        new = list(range(arrived + 1, STAGES[i] + 1))
        last = i == len(loops) - 1
        outs = [jax.ShapeDtypeStruct((8, 128), jnp.int32)]
        outs += [jax.ShapeDtypeStruct((9, rows), jnp.float32)] * (3 * last)
        results = pl.pallas_call(
            functools.partial(pair_kernel, new=new, start=start, steps=steps, unroll=unroll, halved=halved, last=last),
            out_shape=state + outs,
            in_specs=[smem] + [vmem] * (len(new) + 4),
            out_specs=[vmem] * (3 + len(outs)),
            input_output_aliases={2 + len(new) + j: j for j in range(3)},
            compiler_params=pltpu.CompilerParams(vmem_limit_bytes=24 * 2**20),
            cost_estimate=pl.CostEstimate(flops=1000, bytes_accessed=1000, transcendentals=0),
        )(tab, turns[i], *[held[OFFSETS[s]] for s in new], *held_state)
        held_state, finals = results[:3], results[4:]
        turns.append(results[3])
        start += steps * unroll + halved
        arrived = STAGES[i]
    own_part, ahead, behind = finals
    for axis in range(3):
        step = [0, 0, 0]
        step[axis] = 1
        back = [0, 0, 0]
        back[axis] = 3
        ahead = lax.ppermute(ahead, ("clus", "help"), moves(back))
        behind = lax.ppermute(behind, ("clus", "help"), moves(step))
        merged = jnp.maximum(own_part, jnp.maximum(ahead, behind))
        n = merged.shape[0] // 3
        if axis < 2:
            own_part, ahead, behind = merged[:n], merged[n : 2 * n], merged[2 * n :]
    return merged[None]


def solution(mesh):
    in_specs = (P("clus", "help", None, None), P("clus", "help", None), P("clus"))
    out_specs = P("clus", "help", None)
    return jax.shard_map(on_device, mesh=mesh, in_specs=in_specs, out_specs=out_specs, check_vma=False)
```

```python
import functools

import jax
import jax.numpy as jnp
import numpy as np
from jax import lax
from jax.experimental import pallas as pl
from jax.experimental.pallas import tpu as pltpu
from jax.sharding import PartitionSpec as P

EPS = 1e-06
SIDE = 4
UNROLL = 12
FLAG_ROWS = 16
DEAD = -4.0
NORM_PARTS = 2

PLAN = [
    ((0, 1, 0), (0, 0, 0)),
    ((3, 0, 1), (0, 0, 0)),
    ((0, 1, 3), (0, 1, 0)),
    ((3, 3, 0), (0, 0, 0)),
    ((1, 0, 0), (0, 0, 0)),
    ((3, 3, 1), (3, 0, 1)),
    ((3, 1, 1), (3, 0, 1)),
    ((1, 1, 3), (0, 1, 3)),
    ((3, 3, 3), (3, 3, 0)),
    ((1, 0, 1), (1, 0, 0)),
]
OFFSETS = [(0, 0, 0)] + [d for d, _ in PLAN]
STAGES = [2, 4, 5, 7, 9, 10]
GATES = {(0, 1, 3): 0, (1, 1, 3): 1, (1, 0, 1): 2}
AFTER = {(1, 0, 0): (0, 1, 0), (3, 3, 0): (0, 1, 0)}


def turned(d):
    return (-d[0], -d[2], -d[1])


def place_of(v):
    return ((v[0] % SIDE) * SIDE + v[1] % SIDE) * SIDE + v[2] % SIDE


def cube():
    return [(z, y, x) for z in range(SIDE) for y in range(SIDE) for x in range(SIDE)]


def add(a, b):
    return tuple(x + y for x, y in zip(a, b))


def sub(a, b):
    return tuple((x - y) % SIDE for x, y in zip(a, b))


def moves(step):
    pairs = []
    for c in range(2):
        s = turned(step) if c else step
        for v in cube():
            pairs.append((c * SIDE**3 + place_of(add(v, s)), c * SIDE**3 + place_of(v)))
    return pairs


def choose_pairs():
    best = {}
    for a in range(len(OFFSETS)):
        for b in range(a):
            g = sub(OFFSETS[a], OFFSETS[b])
            key = min(g, sub((0, 0, 0), g))
            if key not in best:
                best[key] = (a, b)
    assert len(best) == (SIDE**3 - 1 + 7) // 2
    return sorted(best.values())


def work_table():
    full, halved = [[] for _ in STAGES], [[] for _ in STAGES]
    for a, b in choose_pairs():
        stage = next(i for i, n in enumerate(STAGES) if a <= n)
        twin = all((2 * g) % SIDE == 0 for g in sub(OFFSETS[a], OFFSETS[b]))
        (halved if twin else full)[stage].append((a, b))
    loops, units = [], []
    for f, h in zip(full, halved):
        steps = -(-len(f) // UNROLL)
        unroll = -(-len(f) // max(steps, 1))
        f = f + f[-1:] * (steps * unroll - len(f))
        loops.append((steps, unroll, len(h)))
        units += f + h
    table = np.zeros((2, SIDE**3, len(units) * 3), np.int32)
    for c in range(2):
        offs = [turned(d) if c else d for d in OFFSETS]
        for v in cube():
            for n, (a, b) in enumerate(units):
                first = place_of(add(v, offs[a])) < place_of(add(v, offs[b]))
                k, q = (a, b) if first else (b, a)
                table[c, place_of(v), 3 * n : 3 * n + 3] = (k, q, int(first))
    return table, loops


def unit_kernel(alive, x_hbm, mask_hbm, out_ref, x_ref, mask_ref, sems):
    rows, width = x_ref.shape
    part = rows // NORM_PARTS
    copies = []
    for i in range(NORM_PARTS):
        at = pl.ds(i * part, part)
        copies.append(pltpu.make_async_copy(x_hbm.at[at], x_ref.at[at], sems.at[i]))
        copies[-1].start()
    copies.append(pltpu.make_async_copy(mask_hbm, mask_ref, sems.at[NORM_PARTS]))
    copies[-1].start()
    for i in range(NORM_PARTS):
        copies[i].wait()
        at = slice(i * part, (i + 1) * part)
        x = x_ref[at, :].astype(jnp.float32)
        meansq = jnp.mean(x * x, axis=-1, keepdims=True)
        out_ref[at, :] = (x * lax.rsqrt(meansq + EPS) * (1.0 / width**0.5)).astype(jnp.bfloat16)
    copies[-1].wait()
    live = (mask_ref[...] == 1) & (alive[0] == 1)
    bias = jnp.broadcast_to(jnp.where(live, 0.0, DEAD), (FLAG_ROWS, rows))
    top = lax.broadcasted_iota(jnp.int32, (FLAG_ROWS, rows), 0) == 0
    out_ref[rows:, :] = jnp.zeros((FLAG_ROWS, width), jnp.bfloat16)
    out_ref[rows:, :rows] = jnp.where(top, bias, 0.0).astype(jnp.bfloat16)


def dot_t(a, b):
    return lax.dot_general(a, b, (((1,), (1,)), ((), ())), preferred_element_type=jnp.float32)


def key_bias(flags):
    ones = jnp.ones((flags.shape[0], 128), jnp.bfloat16)
    return lax.dot_general(flags, ones, (((0,), (0,)), ((), ())), preferred_element_type=jnp.float32)


def fold_rows(s):
    n, w = s.shape
    return jnp.max(s.reshape(n // 8, 8, w), axis=0)


def pair_work(tab, at, stack, biases, acc, halved):
    rows = stack.shape[1]
    half = rows // 2
    k, q, h = tab[at], tab[at + 1], tab[at + 2]
    query = stack[q, pl.ds(pl.multiple_of(h * half, half), half), :] if halved else stack[q]
    s = dot_t(stack[k], query)
    s = fold_rows(s + jnp.tile(biases[k], (1, s.shape[1] // 128)))
    if halved:
        acc[q, h] = jnp.maximum(acc[q, h], s)
    else:
        for i in range(2):
            acc[q, i] = jnp.maximum(acc[q, i], s[:, i * half : (i + 1) * half])


def self_kernel(t_ref, tab, stack, biases, acc, turn):
    rows = stack.shape[1]
    half = rows // 2
    stack[0] = t_ref[:rows, :]
    biases[0] = key_bias(t_ref[rows:, :rows])
    acc[...] = jnp.full(acc.shape, -1.0, jnp.float32)
    for h in range(2):
        n = half * (h + 1)
        s = dot_t(t_ref[:n, :], t_ref[h * half : (h + 1) * half, :])
        key = lax.broadcasted_iota(jnp.int32, (n, half), 0)
        query = lax.broadcasted_iota(jnp.int32, (n, half), 1) + h * half
        s = jnp.where(key < query, s + jnp.tile(biases[0, :n], (1, half // 128)), -1.0)
        acc[0, h] = jnp.maximum(acc[0, h], fold_rows(s))
    turn[...] = jnp.full(turn.shape, tab[0], jnp.int32)


def pair_kernel(tab, turn_in, *refs, new, start, steps, unroll, halved, last):
    n = len(new)
    tiles = refs[:n]
    n_out = 3 * last
    stack, biases, acc = refs[n + 3 : n + 6]
    turn = refs[n + 6]
    outs = refs[n + 7 : n + 7 + n_out]
    rows = stack.shape[1]
    half = rows // 2
    flags = jnp.concatenate([t[rows:, :rows] for t in tiles], axis=0)
    shape = (n * FLAG_ROWS, n * 128)
    row, lane = (lax.broadcasted_iota(jnp.int32, shape, a) for a in range(2))
    spread = (row == lane // 128 * FLAG_ROWS).astype(jnp.bfloat16)
    columns = lax.dot_general(flags, spread, (((0,), (0,)), ((), ())), preferred_element_type=jnp.float32)
    for i, slot in enumerate(new):
        biases[slot] = columns[:, i * 128 : (i + 1) * 128]
    for i, slot in enumerate(new):
        stack[slot] = tiles[i][:rows, :]

    def step(u, carry):
        for j in range(unroll):
            pair_work(tab, 3 * (start + u * unroll + j), stack, biases, acc, False)
        return carry

    lax.fori_loop(0, steps, step, 0)
    for j in range(halved):
        pair_work(tab, 3 * (start + steps * unroll + j), stack, biases, acc, True)
    turn[...] = turn_in[...]
    if last:
        for out in outs:
            out[...] = jnp.full(out.shape, -1.0, jnp.float32)
        for s, (z, y, x) in enumerate(OFFSETS):
            row = 3 * (y % 3 + y // 3 * 2) + x % 3 + x // 3 * 2
            for h in range(2):
                outs[z % 3 + z // 3 * 2][row : row + 1, h * half : (h + 1) * half] = jnp.max(
                    acc[s, h], axis=0, keepdims=True
                )


def on_device(embeddings, row_mask, tile_counts):
    rows, width = embeddings.shape[2:]
    half = rows // 2
    clus, place = lax.axis_index("clus"), lax.axis_index("help")
    table, loops = work_table()
    tab = jnp.asarray(table)[clus, place]
    alive = (place < tile_counts).astype(jnp.int32)
    slots = len(OFFSETS)
    vmem, smem, hbm = (pl.BlockSpec(memory_space=m) for m in (pltpu.VMEM, pltpu.SMEM, pltpu.HBM))
    state = [
        pltpu.VMEM((slots, rows, width), jnp.bfloat16),
        pltpu.VMEM((slots, rows, 128), jnp.float32),
        pltpu.VMEM((slots, 2, 8, half), jnp.float32),
    ]

    own = pl.pallas_call(
        unit_kernel,
        out_shape=pltpu.VMEM((rows + FLAG_ROWS, width), jnp.bfloat16),
        in_specs=[smem, hbm, hbm],
        out_specs=vmem,
        scratch_shapes=[
            pltpu.VMEM((rows, width), jnp.bfloat16),
            pltpu.VMEM((1, rows), jnp.int32),
            pltpu.SemaphoreType.DMA((NORM_PARTS + 1,)),
        ],
        compiler_params=pltpu.CompilerParams(vmem_limit_bytes=56 * 2**20),
    )(alive, embeddings[0, 0], row_mask[0])
    *held_state, turn = pl.pallas_call(
        self_kernel,
        out_shape=state + [jax.ShapeDtypeStruct((8, 128), jnp.int32)],
        in_specs=[vmem, smem],
        out_specs=[vmem] * 4,
        compiler_params=pltpu.CompilerParams(vmem_limit_bytes=24 * 2**20),
        cost_estimate=pl.CostEstimate(flops=1000, bytes_accessed=1000, transcendentals=0),
    )(own, tab)
    held = {OFFSETS[0]: own}
    turns = [turn]
    start, arrived = 0, 0
    for d, source in PLAN:
        if d in GATES:
            held[source], turns[GATES[d]] = lax.optimization_barrier((held[source], turns[GATES[d]]))
        sent = held[source]
        if d in AFTER:
            sent, held[AFTER[d]] = lax.optimization_barrier((sent, held[AFTER[d]]))
        held[d] = lax.ppermute(sent, ("clus", "help"), moves(sub(d, source)))
        i = len(turns) - 1
        if len(held) - 1 < STAGES[i]:
            continue
        steps, unroll, halved = loops[i]
        new = list(range(arrived + 1, STAGES[i] + 1))
        last = i == len(loops) - 1
        outs = [jax.ShapeDtypeStruct((8, 128), jnp.int32)]
        outs += [jax.ShapeDtypeStruct((9, rows), jnp.float32)] * (3 * last)
        results = pl.pallas_call(
            functools.partial(pair_kernel, new=new, start=start, steps=steps, unroll=unroll, halved=halved, last=last),
            out_shape=state + outs,
            in_specs=[smem] + [vmem] * (len(new) + 4),
            out_specs=[vmem] * (3 + len(outs)),
            input_output_aliases={2 + len(new) + j: j for j in range(3)},
            compiler_params=pltpu.CompilerParams(vmem_limit_bytes=24 * 2**20),
            cost_estimate=pl.CostEstimate(flops=1000, bytes_accessed=1000, transcendentals=0),
        )(tab, turns[i], *[held[OFFSETS[s]] for s in new], *held_state)
        held_state, finals = results[:3], results[4:]
        turns.append(results[3])
        start += steps * unroll + halved
        arrived = STAGES[i]
    own_part, ahead, behind = finals
    for axis in range(3):
        step = [0, 0, 0]
        step[axis] = 1
        back = [0, 0, 0]
        back[axis] = 3
        ahead = lax.ppermute(ahead, ("clus", "help"), moves(back))
        behind = lax.ppermute(behind, ("clus", "help"), moves(step))
        merged = jnp.maximum(own_part, jnp.maximum(ahead, behind))
        n = merged.shape[0] // 3
        if axis < 2:
            own_part, ahead, behind = merged[:n], merged[n : 2 * n], merged[2 * n :]
    return merged[None]


def solution(mesh):
    in_specs = (P("clus", "help", None, None), P("clus", "help", None), P("clus"))
    out_specs = P("clus", "help", None)
    return jax.shard_map(on_device, mesh=mesh, in_specs=in_specs, out_specs=out_specs, check_vma=False)
```
